32 devices in a mesh: parts: 2 (over x), row: 16 (over z, y, core).
Axes of the slice: x: 2, y: 2, z: 4, core: 2. Of those that a mesh axis runs over, the one named last changes fastest.
Arguments:
- features: bfloat16 [8192, 256], P(('parts', 'row')), parts along dimension 0, may hold values from -6 to 6
- weight: bfloat16 [256, 256], replicated, may hold values from -0.375 to 0.375
- bias: float32 [256], replicated, may hold values from -3 to 3
- tiles: bfloat16 [2048, 256, 256], P(('parts', 'row')), parts along dimension 0, may hold values from -0.15625 to 0.15625
- tile_col: int32 [32, 64], P(('parts', 'row')), parts along dimension 0, may hold values from 0 to 15
- live_tiles: int32 [32], P(('parts', 'row')), parts along dimension 0, may hold values from 1 to 64, 512 in all
- cotangent: bfloat16 [8192, 256], P(('parts', 'row')), parts along dimension 0, may hold values from -6 to 6
Outputs:
- activation: bfloat16 [8192, 256], P(('parts', 'row')), parts along dimension 0
- grad_features: bfloat16 [8192, 256], P(('parts', 'row')), parts along dimension 0
- grad_weight: float32 [512, 256], P('parts'), parts along dimension 0
- grad_bias: float32 [512], P('parts'), parts along dimension 0
The draws below stay inside these ranges and needn't reach their ends.
There are 2 independent parts, one for each index of `parts`. The reference program is written for one: setup_inputs(seed, part) draws one part's arguments, and reference() takes and returns one part's arrays. A program takes and returns all parts, laid end to end along the dimension named above; an argument that names none is the same for every part. Nothing has to cross between parts.
Inputs may be any that keep to these rules, and one draw needn't show every extreme that they name: `live_tiles`: the counts sum to 16 * 32 and one block row reaches 64.
All inputs are finite; a program needn't handle non-finite values.
Results may differ from the reference program's by a relative error of at most 0.007.
Values may be sent and summed in bfloat16 or wider, within the bound.
No kernel may reach another device: no remote copies, remote signals or barrier semaphores. Data moves between devices by JAX's collectives and lax.ppermute only.
A program may use at most 128 MiB of HBM per device.

```python
import math
import jax
import jax.numpy as jnp
import numpy as np
from jax import lax

F = 256
TILE = 256
TMAX = 64
NODES = 4096
N_ROW = 16


def with_ends(result, rng, least, largest):
    longest = result.shape.index(max(result.shape))
    spots = []
    for shift in (0, 1):
        where = [jax.random.randint(jax.random.fold_in(rng, axis), (), 0, length) for axis, length in enumerate(result.shape)]
        where[longest] = (where[longest] + shift) % result.shape[longest]
        spots.append(tuple(where))
    return result.at[spots[0]].set(least).at[spots[1]].set(largest)


def levels(key, shape, split, least, largest):
    def one(dim, blocks):
        heights = jax.random.uniform(jax.random.fold_in(jax.random.fold_in(key, 6), dim), (blocks,), jnp.float32, least / len(split), largest / len(split))
        return jnp.repeat(jnp.exp(heights), shape[dim] // blocks).reshape((-1,) + (1,) * (len(shape) - dim - 1))

    factor_of = one(*split[0])
    for cut in split[1:]:
        factor_of = factor_of * one(*cut)
    return factor_of


def split_up(amount, total, most, slope):
    weights = [(1 << 20) // math.isqrt(rank ** slope) + 1 for rank in range(2, amount + 1)]
    surplus, counts = total - most - (amount - 1), [1] * (amount - 1)
    while surplus > 0:
        candidates = [i for i in range(amount - 1) if counts[i] < most]
        pool, budget = sum([weights[i] for i in candidates]), surplus
        for i in candidates:
            extra = min(most - counts[i], max(1, budget * weights[i] // pool), surplus)
            counts[i] = counts[i] + extra
            surplus = surplus - extra
    return np.array([most] + counts)


def ragged(key, number_of, total, reach, skew):
    if number_of == 2:
        one = jax.random.randint(key, (), max(1, total - reach), min(reach, total - 1) + 1)
        return jnp.stack([one, total - one])
    lengths = jnp.asarray(split_up(number_of, total, reach, skew), jnp.int32)
    couples = (number_of - 1) // 2
    source_of, taker = lengths[1:1 + 2 * couples:2], lengths[2:2 + 2 * couples:2]
    margin = jnp.minimum(source_of - 1, reach - taker)
    passed = jax.random.randint(jax.random.fold_in(key, 1), (couples,), 0, 1 << 20) % (margin + 1)
    lengths = lengths.at[1:1 + 2 * couples:2].set(source_of - passed).at[2:2 + 2 * couples:2].set(taker + passed)
    return lengths[jax.random.permutation(jax.random.fold_in(key, 2), number_of)]


def normal_values(key, extent, spread, limit, cuts=(), kind=jnp.bfloat16):
    drawn = spread * jax.random.normal(key, extent, jnp.float32)
    if cuts:
        drawn = drawn * levels(key, extent, cuts, -0.22, 0.18)
    return jnp.clip(drawn, -limit, limit).astype(kind)


def setup_inputs(seed: int = 0, part: int = 0) -> dict:
    keys = jax.random.split(jax.random.key(seed), 8)
    own_keys = jax.random.split(jax.random.fold_in(keys[7], part), 8)
    features = normal_values(own_keys[0], (NODES, F), 1.0, 6.0, ((0, 16),))
    weight = normal_values(keys[1], (F, F), F ** -0.5, 0.375)
    bias = normal_values(keys[2], (F,), 0.5, 3.0, (), jnp.float32)
    tiles = normal_values(own_keys[3], (N_ROW * TMAX, TILE, TILE), ((2.0 / (TMAX * TILE)) ** 0.5), 0.15625, ((0, 16),))
    tile_col = with_ends(jax.random.randint(own_keys[4], (N_ROW, TMAX), 0, N_ROW), jax.random.fold_in(own_keys[4], 1), 0, N_ROW - 1).astype(jnp.int32)
    live_tiles = ragged(own_keys[5], N_ROW, N_ROW * TMAX // 2, TMAX, 2).astype(jnp.int32)
    cotangent = normal_values(own_keys[6], (NODES, F), 1.0, 6.0, ((0, 16),))
    return dict(features=features, weight=weight, bias=bias, tiles=tiles, tile_col=tile_col, live_tiles=live_tiles, cotangent=cotangent)


def merged_blocks(tiles_row, columns, count):
    slot_ids = jnp.arange(TMAX, dtype=jnp.int32)
    live = slot_ids < count
    same = columns[:, None] == columns[None, :]
    earlier = slot_ids[None, :] < slot_ids[:, None]
    repeated = jnp.any(same & earlier & live[None, :], axis=1)
    first = live & jnp.logical_not(repeated)
    merge = (same & first[:, None] & live[None, :]).astype(jnp.float32)
    return jnp.einsum('st,tab->sab', merge, tiles_row.astype(jnp.float32)).astype(jnp.bfloat16)


def reference(features, weight, bias, tiles, tile_col, live_tiles, cotangent):
    projected = jnp.dot(features, weight, preferred_element_type=jnp.float32).astype(jnp.bfloat16)
    blocks = projected.reshape(N_ROW, TILE, F)
    tiles_rows = tiles.reshape(N_ROW, TMAX, TILE, TILE)

    def forward_block(index):
        compact = merged_blocks(tiles_rows[index], tile_col[index], live_tiles[index])
        chosen = blocks[tile_col[index]].astype(jnp.float32)
        return jnp.einsum('sab,sbf->af', compact.astype(jnp.float32), chosen)

    aggregate = lax.map(forward_block, jnp.arange(N_ROW, dtype=jnp.int32)).reshape(NODES, F)
    pre = aggregate + bias[None, :]
    sigma = jax.nn.sigmoid(pre)
    activation = (pre * sigma).astype(jnp.bfloat16)
    grad_pre = (cotangent.astype(jnp.float32) * sigma * (1.0 + pre * (1.0 - sigma))).astype(jnp.bfloat16)
    grad_blocks = grad_pre.reshape(N_ROW, TILE, F)

    def backward_step(total, index):
        compact = merged_blocks(tiles_rows[index], tile_col[index], live_tiles[index])
        contrib = jnp.einsum('sab,af->sbf', compact.astype(jnp.float32), grad_blocks[index].astype(jnp.float32))
        return total.at[tile_col[index]].add(contrib), None

    total, unused = lax.scan(backward_step, jnp.zeros((N_ROW, TILE, F), jnp.float32), jnp.arange(N_ROW, dtype=jnp.int32))
    grad_projected = total.reshape(NODES, F).astype(jnp.bfloat16)
    grad_weight = jnp.dot(features.T, grad_projected, preferred_element_type=jnp.float32)
    grad_bias = jnp.sum(grad_pre.astype(jnp.float32), axis=0)
    grad_features = jnp.dot(grad_projected, weight.T, preferred_element_type=jnp.float32).astype(jnp.bfloat16)
    return activation, grad_features, grad_weight, grad_bias
```

```python
import functools

import jax
import jax.numpy as jnp
from jax import lax
from jax.experimental import pallas as pl
from jax.experimental.pallas import tpu as pltpu
from jax.sharding import PartitionSpec as P

F32 = jnp.float32
BF16 = jnp.bfloat16
VMEM = pl.BlockSpec(memory_space=pltpu.VMEM)
SMEM = pl.BlockSpec(memory_space=pltpu.SMEM)
LIMIT = 48 * 1024 * 1024


def dot(a, b):
    return jnp.dot(a, b, preferred_element_type=F32)


def halves(x):
    high = x.astype(BF16)
    return high, (x - high.astype(F32)).astype(BF16)


def call(kernel, out_shape, args, in_specs=None, scratch=(), flops=0, moved=0):
    many = isinstance(out_shape, (list, tuple))
    return pl.pallas_call(
        kernel,
        out_shape=out_shape,
        in_specs=in_specs or [VMEM] * len(args),
        out_specs=[VMEM] * len(out_shape) if many else VMEM,
        scratch_shapes=list(scratch),
        compiler_params=pltpu.CompilerParams(vmem_limit_bytes=LIMIT),
        cost_estimate=pl.CostEstimate(flops=flops, bytes_accessed=moved, transcendentals=0),
    )(*args)


def merge_kernel(columns, live, me, tiles, own, other, held, total, sems):
    count = live[0]
    blocks = total.shape[0]

    def fetch(slot):
        return pltpu.make_async_copy(tiles.at[slot], held.at[slot], sems.at[slot])

    def start(slot, carry):
        fetch(slot).start()
        return carry

    lax.fori_loop(0, count, start, 0)

    def clear(index, carry):
        total[index] = jnp.zeros(total.shape[1:], F32)
        return carry

    lax.fori_loop(0, blocks, clear, 0)

    def add(slot, carry):
        fetch(slot).wait()
        where = lax.bitwise_xor(columns[slot], me[0])
        total[where] += held[slot].astype(F32)
        return carry

    lax.fori_loop(0, count, add, 0)

    def store(index, carry):
        own[index] = total[2 * index].astype(BF16)
        other[index] = total[2 * index + 1].astype(BF16)
        return carry

    lax.fori_loop(0, blocks // 2, store, 0)


def aggregate_kernel(own, other, *refs):
    xs, (mine, partner) = refs[:-2], refs[-2:]
    total_mine = jnp.zeros(mine.shape, F32)
    total_partner = jnp.zeros(mine.shape, F32)
    for index, x in enumerate(xs):
        total_mine += dot(own[index], x[...])
        total_partner += dot(other[index], x[...])
    mine[...] = total_mine
    partner[...] = total_partner


def layer_kernel(mine, received, weight, bias, cotangent, activation, grad_pre_t, grad_bias):
    high, low = halves(mine[...] + received[...])
    pre = dot(high, weight[...]) + dot(low, weight[...]) + bias[...]
    sigma = jax.nn.sigmoid(pre)
    activation[...] = (pre * sigma).astype(BF16)
    grad = (cotangent[...].astype(F32) * sigma * (1.0 + pre * (1.0 - sigma))).astype(BF16)
    grad = grad.astype(F32)
    grad_bias[...] = jnp.broadcast_to(jnp.sum(grad, axis=0, keepdims=True), grad_bias.shape)
    grad_pre_t[...] = grad.T.astype(BF16)


def backward_kernel(groups, core, own, other, grad, grad_other, mine, partner, grad_bias, *refs):
    sends, (keep, weight_keep, weight_send, whole) = refs[:len(groups)], refs[len(groups):]
    g, go = grad[...], grad_other[...]
    place = 0
    for send, group in zip(sends, groups):
        for slot, z in enumerate(group):
            at = z // 2
            send[slot] = (dot(g, own[at + 1]) + dot(go, other[at + 1])).astype(BF16)
            keep[place] = dot(g, own[at]) + dot(go, other[at])
            place += 1
    high, low = halves(mine[...])
    high_o, low_o = halves(partner[...])
    whole[...] = (dot(g, high) + dot(g, low) + dot(go, high_o) + dot(go, low_o)).T
    half = weight_keep.shape[0] - 8
    for out, which in ((weight_keep, core[0]), (weight_send, 1 - core[0])):
        out[pl.ds(0, half), :] = whole[pl.ds(pl.multiple_of(which * half, half), half), :]
        out[pl.ds(half, 8), :] = grad_bias[...]


def finish_kernel(kept, from_y, *refs):
    arrived, (weight, grad_features) = refs[:-2], refs[-2:]
    total = kept[...] + from_y[...].astype(F32)
    for part in arrived:
        total += part[...].astype(F32)
    grad_features[...] = lax.dot_general(
        total.T.astype(BF16), weight[...], (((1,), (1,)), ((), ())), preferred_element_type=F32
    ).astype(BF16)


def on_device(features, weight, bias, tiles, tile_col, live_tiles, cotangent):
    side, width = features.shape
    slots = tiles.shape[0]
    count = lax.axis_size("row")
    pairs = count // 2
    me = lax.axis_index("row").astype(jnp.int32)
    core = jnp.bitwise_and(me, 1)

    def swap(x, bit):
        return lax.ppermute(x, "row", [(i, i ^ bit) for i in range(count)])

    block = (side, width)
    own, send_other = call(
        merge_kernel,
        [jax.ShapeDtypeStruct((pairs, side, side), BF16)] * 2,
        (tile_col[0], live_tiles, me[None], tiles),
        in_specs=[SMEM, SMEM, SMEM, pl.BlockSpec(memory_space=pl.ANY)],
        scratch=[
            pltpu.VMEM((slots, side, side), BF16),
            pltpu.VMEM((count, side, side), F32),
            pltpu.SemaphoreType.DMA((slots,)),
        ],
        flops=slots * side * side,
        moved=slots * side * side * 2,
    )
    zs = list(range(count - 4, -4, -4))
    gathered = {0: features}
    for z in zs[:-1]:
        gathered[z] = swap(features, z)
    gathered[2] = swap(features, 2)
    for z in reversed(zs[:-1]):
        gathered[z + 2] = swap(gathered[z], 2)
    other = swap(send_other, 1)
    xs = [gathered[2 * index] for index in range(pairs)]
    mine, partner = call(
        aggregate_kernel,
        [jax.ShapeDtypeStruct(block, F32)] * 2,
        (own, other, *xs),
        flops=4 * pairs * side**2 * width,
        moved=3 * pairs * side * width * 2,
    )
    received = swap(partner, 1)
    activation, grad, grad_bias = call(
        layer_kernel,
        [
            jax.ShapeDtypeStruct(block, BF16),
            jax.ShapeDtypeStruct((width, side), BF16),
            jax.ShapeDtypeStruct((8, width), F32),
        ],
        (mine, received, weight, bias[None, :], cotangent),
        flops=4 * side * width**2,
        moved=side * width * 16,
    )
    grad_other = swap(grad, 1)
    middle = (len(zs) + 1) // 2
    groups = [zs[:middle], zs[middle:]]
    half = jax.ShapeDtypeStruct((width // 2 + 8, width), F32)
    *sends, keep, weight_keep, weight_send = call(
        functools.partial(backward_kernel, groups),
        [jax.ShapeDtypeStruct((len(group), width, side), BF16) for group in groups]
        + [jax.ShapeDtypeStruct((len(zs), width, side), F32), half, half],
        (core[None], own, other, grad, grad_other, mine, partner, grad_bias),
        in_specs=[SMEM] + [VMEM] * 7,
        scratch=[pltpu.VMEM((width, width), F32)],
        flops=4 * pairs * side**2 * width,
        moved=3 * pairs * side * width * 2,
    )
    arrived = []
    place = 0
    from_y = [swap(send, 2) for send in sends]
    for group, received_y in zip(groups, from_y):
        for slot, z in enumerate(group):
            if z:
                summed = (keep[place] + received_y[slot].astype(F32)).astype(BF16)
                arrived.append(swap(summed, z))
            place += 1
    part = weight_keep + swap(weight_send, 1)
    bit = 2
    while bit < count:
        part = part + swap(part, bit)
        bit *= 2
    mine_w = part[: width // 2]
    other_w = swap(mine_w, 1)
    grad_weight = jnp.where(
        core == 0, jnp.concatenate([mine_w, other_w]), jnp.concatenate([other_w, mine_w])
    )
    grad_features = call(
        finish_kernel,
        jax.ShapeDtypeStruct(block, BF16),
        (keep[-1], from_y[-1][-1], *arrived, weight),
        flops=2 * side * width**2,
        moved=side * width * 2 * (len(zs) + 4),
    )
    return activation, grad_features, grad_weight, part[width // 2]


def solution(mesh):
    placed = (
        P(("parts", "row"), None),
        P(),
        P(),
        P(("parts", "row"), None, None),
        P(("parts", "row"), None),
        P(("parts", "row")),
        P(("parts", "row"), None),
    )
    return jax.shard_map(
        on_device,
        mesh=mesh,
        in_specs=placed,
        out_specs=(
            P(("parts", "row"), None),
            P(("parts", "row"), None),
            P("parts", None),
            P("parts"),
        ),
        check_vma=False,
    )
```

```python
import functools

import jax
import jax.numpy as jnp
from jax import lax
from jax.experimental import pallas as pl
from jax.experimental.pallas import tpu as pltpu
from jax.sharding import PartitionSpec as P

F32 = jnp.float32
BF16 = jnp.bfloat16
VMEM = pl.BlockSpec(memory_space=pltpu.VMEM)
SMEM = pl.BlockSpec(memory_space=pltpu.SMEM)
MIB = 1024 * 1024
PIECES = 8
JOIN = 20000000


def dot(a, b):
    return jnp.dot(a, b, preferred_element_type=F32)


def halves(x):
    high = x.astype(BF16)
    return high, (x - high.astype(F32)).astype(BF16)


def at(pieces, index):
    depth = pieces[0].shape[0]
    return pieces[index // depth][index % depth]


def call(kernel, out_shape, args, in_specs=None, scratch=(), flops=0, moved=0, limit=8):
    many = isinstance(out_shape, (list, tuple))
    return pl.pallas_call(
        kernel,
        out_shape=out_shape,
        in_specs=in_specs or [VMEM] * len(args),
        out_specs=[VMEM] * len(out_shape) if many else VMEM,
        scratch_shapes=list(scratch),
        compiler_params=pltpu.CompilerParams(vmem_limit_bytes=limit * MIB),
        cost_estimate=pl.CostEstimate(flops=flops, bytes_accessed=moved, transcendentals=0),
    )(*args)


def merge_kernel(parity, columns, live, me, tiles, *refs):
    others, (held, head, following, sems) = refs[:-4], refs[-4:]
    depth, side = others[0].shape[:2]
    strip = side // 4

    def clear(index, carry):
        head[index] = -1
        return carry

    lax.fori_loop(0, head.shape[0], clear, 0)

    def link(slot, carry):
        where = lax.bitwise_xor(columns[slot], me[0])
        following[slot] = head[where]
        head[where] = slot
        return carry

    lax.fori_loop(0, live[0], link, 0)

    def fetch(slot):
        return pltpu.make_async_copy(tiles.at[slot], held.at[slot], sems.at[slot])

    def chain(index, act):
        def step(slot):
            act(fetch(slot))
            return following[slot]

        lax.while_loop(lambda slot: slot >= 0, step, head[index])

    outs = [(parity + 2 * depth * index, out) for index, out in enumerate(others)]

    def start(base, index, carry):
        chain(2 * index + base, lambda copy: copy.start())
        return carry

    def fill(base, out, index, carry):
        chain(2 * index + base, lambda copy: copy.wait())
        for part in range(4):
            rows = pl.ds(part * strip, strip)

            def add(state, rows=rows):
                slot, total = state
                return following[slot], total + held[slot, rows, :].astype(F32)

            first = (head[2 * index + base], jnp.zeros((strip, side), F32))
            total = lax.while_loop(lambda state: state[0] >= 0, add, first)[1]
            out[index, rows, :] = total.astype(BF16)
        return carry

    for base, out in outs:
        lax.fori_loop(0, out.shape[0], functools.partial(start, base), 0)
    for base, out in outs:
        lax.fori_loop(0, out.shape[0], functools.partial(fill, base, out), 0)


def aggregate_kernel(own, *refs):
    xs, (mine, partner) = refs[PIECES:-2], refs[-2:]
    total_mine = jnp.zeros(mine.shape, F32)
    total_partner = jnp.zeros(mine.shape, F32)
    for index, x in enumerate(xs):
        total_mine += dot(own[index], x[...])
        total_partner += dot(at(refs[:PIECES], index), x[...])
    mine[...] = total_mine
    partner[...] = total_partner


def layer_kernel(mine, received, weight, bias, cotangent, activation, grad_pre_t, grad_bias):
    high, low = halves(mine[...] + received[...])
    pre = dot(high, weight[...]) + dot(low, weight[...]) + bias[...]
    sigma = jax.nn.sigmoid(pre)
    activation[...] = (pre * sigma).astype(BF16)
    grad = (cotangent[...].astype(F32) * sigma * (1.0 + pre * (1.0 - sigma))).astype(BF16)
    grad = grad.astype(F32)
    grad_bias[...] = jnp.broadcast_to(jnp.sum(grad, axis=0, keepdims=True), grad_bias.shape)
    grad_pre_t[...] = grad.T.astype(BF16)


def weight_kernel(core, mine, received, grad, grad_bias, keep, send, whole):
    high, low = halves(mine[...] + received[...])
    whole[...] = (dot(grad[...], high) + dot(grad[...], low)).T
    half = keep.shape[0] - 8
    for out, which in ((keep, core[0]), (send, 1 - core[0])):
        out[pl.ds(0, half), :] = whole[pl.ds(pl.multiple_of(which * half, half), half), :]
        out[pl.ds(half, 8), :] = grad_bias[...]


def backward_kernel(groups, own, grad, grad_other, *refs):
    other, refs = refs[:PIECES], refs[PIECES:]
    sends, keeps = refs[: len(groups)], refs[len(groups) :]
    g, go = grad[...], grad_other[...]
    place = 0
    for send, group in zip(sends, groups):
        for slot, z in enumerate(group):
            near, far = z // 2, z // 2 + 1
            send[slot] = (dot(g, own[far]) + dot(go, at(other, far))).astype(BF16)
            keeps[place][...] = dot(g, own[near]) + dot(go, at(other, near))
            place += 1


def join_kernel(amount, late, *refs):
    refs = refs[late:]
    keeps, received, refs = refs[:amount], refs[amount], refs[amount + 1 :]
    outs = refs[-amount:] if len(refs) == amount else refs[2:-1]
    for slot in range(amount):
        summed = keeps[slot][...] + received[slot].astype(F32)
        outs[slot][...] = summed.astype(outs[slot].dtype)
    if len(refs) > amount:
        refs[-1][...] = refs[0][...] + refs[1][...]


def finish_kernel(core, kept, *refs):
    arrived, refs = refs[:-6], refs[-6:]
    weight, part, part_other, grad_features, grad_weight, grad_bias = refs
    total = kept[...]
    for piece in arrived:
        total += piece[...].astype(F32)
    grad_features[...] = lax.dot_general(
        total.T.astype(BF16), weight[...], (((1,), (1,)), ((), ())), preferred_element_type=F32
    ).astype(BF16)
    half = part_other.shape[0]
    grad_weight[pl.ds(pl.multiple_of(core[0] * half, half), half), :] = part[pl.ds(0, half), :]
    grad_weight[pl.ds(pl.multiple_of((1 - core[0]) * half, half), half), :] = part_other[...]
    grad_bias[...] = part[pl.ds(half, 1), :]


def on_device(features, weight, bias, tiles, tile_col, live_tiles, cotangent):
    side, width = features.shape
    slots = tiles.shape[0]
    count = lax.axis_size("row")
    pairs = count // 2
    me = lax.axis_index("row").astype(jnp.int32)
    core = jnp.bitwise_and(me, 1)

    def swap(x, bit):
        return lax.ppermute(x, "row", [(i, i ^ bit) for i in range(count)])

    block = (side, width)
    wide = jax.ShapeDtypeStruct(block, F32)
    wide_t = jax.ShapeDtypeStruct((width, side), F32)
    zs = list(range(count - 4, -4, -4))
    gathered = {0: features}
    for z in zs[:-1]:
        gathered[z] = swap(features, z)
    gathered[2] = swap(features, 2)
    def merge(parity, pieces):
        return call(
            functools.partial(merge_kernel, parity),
            [jax.ShapeDtypeStruct((pairs // pieces, side, side), BF16)] * pieces,
            (tile_col[0], live_tiles, me[None], tiles),
            in_specs=[SMEM, SMEM, SMEM, pl.BlockSpec(memory_space=pl.ANY)],
            scratch=[
                pltpu.VMEM((slots, side, side), BF16),
                pltpu.SMEM((count,), jnp.int32),
                pltpu.SMEM((slots,), jnp.int32),
                pltpu.SemaphoreType.DMA((slots,)),
            ],
            flops=slots * side * side,
            moved=slots * side * side,
            limit=48,
        )

    (own,) = merge(0, 1)
    sent_other = merge(1, PIECES)
    for z in reversed(zs[:-1]):
        gathered[z + 2] = swap(gathered[z], 2)
    other = [swap(piece, 1) for piece in sent_other]
    xs = [gathered[2 * index] for index in range(pairs)]
    mine, partner = call(
        aggregate_kernel,
        [wide] * 2,
        (own, *other, *xs),
        flops=4 * pairs * side**2 * width,
        moved=3 * pairs * side * width * 2,
    )
    received = swap(partner, 1)
    activation, grad, grad_bias = call(
        layer_kernel,
        [
            jax.ShapeDtypeStruct(block, BF16),
            jax.ShapeDtypeStruct((width, side), BF16),
            jax.ShapeDtypeStruct((8, width), F32),
        ],
        (mine, received, weight, bias[None, :], cotangent),
        flops=4 * side * width**2,
        moved=side * width * 16,
    )
    grad_other = swap(grad, 1)
    half = jax.ShapeDtypeStruct((width // 2 + 8, width), F32)
    part, part_send = call(
        weight_kernel,
        [half] * 2,
        (core[None], mine, received, grad, grad_bias),
        in_specs=[SMEM] + [VMEM] * 4,
        scratch=[pltpu.VMEM((width, width), F32)],
        flops=4 * side * width**2,
        moved=side * width * 12,
    )
    part = part + swap(part_send, 1)
    bits = []
    while 2 << len(bits) < count:
        bits.insert(0, 2 << len(bits))
    share = max(1, len(zs) // 4)
    groups = [zs[:share], zs[share : 2 * share], zs[2 * share :]]
    outs = call(
        functools.partial(backward_kernel, groups),
        [jax.ShapeDtypeStruct((len(group), width, side), BF16) for group in groups]
        + [wide_t] * len(zs),
        (own, grad, grad_other, *other),
        flops=4 * pairs * side**2 * width,
        moved=3 * pairs * side * width * 2,
    )
    sends, keeps = outs[: len(groups)], outs[len(groups) :]
    from_y = [swap(send, 2) for send in sends]
    arrived = []
    place = 0
    for index, group in enumerate(groups):
        shapes = [jax.ShapeDtypeStruct((width, side), BF16 if z else F32) for z in group]
        args = [*keeps[place : place + len(group)], from_y[index]]
        if index != 1:
            shapes.append(half)
            args += [part, swap(part, bits.pop(0))]
        if index == 2:
            args.insert(0, summed[0])
        *summed, = call(
            functools.partial(join_kernel, len(group), index == 2),
            shapes,
            args,
            flops=len(group) * side * width,
            in_specs=[pl.BlockSpec(memory_space=pl.ANY)] * (index == 2) + [VMEM] * (len(args) - (index == 2)),
            moved=JOIN,
        )
        if index != 1:
            part = summed.pop()
        arrived += [swap(piece, z) if z else piece for piece, z in zip(summed, group)]
        place += len(group)
    for bit in bits:
        part = part + swap(part, bit)
    part_other = swap(part[: width // 2], 1)
    grad_features, grad_weight, grad_bias = call(
        finish_kernel,
        [
            jax.ShapeDtypeStruct(block, BF16),
            jax.ShapeDtypeStruct((width, width), F32),
            jax.ShapeDtypeStruct((1, width), F32),
        ],
        (core[None], arrived[-1], *arrived[:-1], weight, part, part_other),
        in_specs=[SMEM] + [VMEM] * (len(zs) + 3),
        flops=2 * side * width**2,
        moved=side * width * 2 * (len(zs) + 4),
    )
    return activation, grad_features, grad_weight, grad_bias[0]


def solution(mesh):
    placed = (
        P(("parts", "row"), None),
        P(),
        P(),
        P(("parts", "row"), None, None),
        P(("parts", "row"), None),
        P(("parts", "row")),
        P(("parts", "row"), None),
    )
    return jax.shard_map(
        on_device,
        mesh=mesh,
        in_specs=placed,
        out_specs=(
            P(("parts", "row"), None),
            P(("parts", "row"), None),
            P("parts", None),
            P("parts"),
        ),
        check_vma=False,
    )
```

```python
import functools

import jax
import jax.numpy as jnp
from jax import lax
from jax.experimental import pallas as pl
from jax.experimental.pallas import tpu as pltpu
from jax.sharding import PartitionSpec as P

F32 = jnp.float32
BF16 = jnp.bfloat16
VMEM = pl.BlockSpec(memory_space=pltpu.VMEM)
SMEM = pl.BlockSpec(memory_space=pltpu.SMEM)
MIB = 1024 * 1024
PIECES = 8


def dot(a, b):
    return jnp.dot(a, b, preferred_element_type=F32)


def halves(x):
    high = x.astype(BF16)
    return high, (x - high.astype(F32)).astype(BF16)


def at(pieces, index):
    depth = pieces[0].shape[0]
    return pieces[index // depth][index % depth]


def call(kernel, out_shape, args, in_specs=None, scratch=(), flops=0, moved=0, limit=8):
    many = isinstance(out_shape, (list, tuple))
    return pl.pallas_call(
        kernel,
        out_shape=out_shape,
        in_specs=in_specs or [VMEM] * len(args),
        out_specs=[VMEM] * len(out_shape) if many else VMEM,
        scratch_shapes=list(scratch),
        compiler_params=pltpu.CompilerParams(vmem_limit_bytes=limit * MIB),
        cost_estimate=pl.CostEstimate(flops=flops, bytes_accessed=moved, transcendentals=0),
    )(*args)


def merge_kernel(parity, columns, live, me, tiles, *refs):
    others, (held, head, following, sems) = refs[:-4], refs[-4:]
    depth, side = others[0].shape[:2]
    strip = side // 4

    def clear(index, carry):
        head[index] = -1
        return carry

    lax.fori_loop(0, head.shape[0], clear, 0)

    def link(slot, carry):
        where = lax.bitwise_xor(columns[slot], me[0])
        following[slot] = head[where]
        head[where] = slot
        return carry

    lax.fori_loop(0, live[0], link, 0)

    def fetch(slot):
        return pltpu.make_async_copy(tiles.at[slot], held.at[slot], sems.at[slot])

    def chain(index, act):
        def step(slot):
            act(fetch(slot))
            return following[slot]

        lax.while_loop(lambda slot: slot >= 0, step, head[index])

    outs = [(parity + 2 * depth * index, out) for index, out in enumerate(others)]

    def start(base, index, carry):
        chain(2 * index + base, lambda copy: copy.start())
        return carry

    def fill(base, out, index, carry):
        chain(2 * index + base, lambda copy: copy.wait())
        for part in range(4):
            rows = pl.ds(part * strip, strip)

            def add(state, rows=rows):
                slot, total = state
                return following[slot], total + held[slot, rows, :].astype(F32)

            first = (head[2 * index + base], jnp.zeros((strip, side), F32))
            total = lax.while_loop(lambda state: state[0] >= 0, add, first)[1]
            out[index, rows, :] = total.astype(BF16)
        return carry

    for base, out in outs:
        lax.fori_loop(0, out.shape[0], functools.partial(start, base), 0)
    for base, out in outs:
        lax.fori_loop(0, out.shape[0], functools.partial(fill, base, out), 0)


def aggregate_kernel(own, *refs):
    xs, (mine, partner) = refs[PIECES:-2], refs[-2:]
    total_mine = jnp.zeros(mine.shape, F32)
    total_partner = jnp.zeros(mine.shape, F32)
    for index, x in enumerate(xs):
        total_mine += dot(own[index], x[...])
        total_partner += dot(at(refs[:PIECES], index), x[...])
    mine[...] = total_mine
    partner[...] = total_partner


def layer_kernel(mine, received, weight, bias, cotangent, activation, grad_pre_t, grad_bias):
    high, low = halves(mine[...] + received[...])
    pre = dot(high, weight[...]) + dot(low, weight[...]) + bias[...]
    sigma = jax.nn.sigmoid(pre)
    activation[...] = (pre * sigma).astype(BF16)
    grad = (cotangent[...].astype(F32) * sigma * (1.0 + pre * (1.0 - sigma))).astype(BF16)
    grad = grad.astype(F32)
    grad_bias[...] = jnp.broadcast_to(jnp.sum(grad, axis=0, keepdims=True), grad_bias.shape)
    grad_pre_t[...] = grad.T.astype(BF16)


def weight_kernel(core, mine, received, grad, grad_bias, keep, send, whole):
    high, low = halves(mine[...] + received[...])
    whole[...] = (dot(grad[...], high) + dot(grad[...], low)).T
    half = keep.shape[0] - 16
    for out, which in ((keep, core[0]), (send, 1 - core[0])):
        out[pl.ds(0, half), :] = whole[pl.ds(pl.multiple_of(which * half, half), half), :]
        out[pl.ds(half, 8), :] = grad_bias[...]
        out[pl.ds(half + 8, 8), :] = jnp.zeros_like(grad_bias)


def backward_kernel(groups, own, grad, grad_other, *refs):
    other, refs = refs[:PIECES], refs[PIECES:]
    sends, keeps = refs[: len(groups)], refs[len(groups) :]
    g, go = grad[...], grad_other[...]
    place = 0
    for send, group in zip(sends, groups):
        for slot, z in enumerate(group):
            near, far = z // 2, z // 2 + 1
            send[slot] = (dot(g, own[far]) + dot(go, at(other, far))).astype(BF16)
            keeps[place][...] = dot(g, own[near]) + dot(go, at(other, near))
            place += 1


def join_kernel(keeps_amount, *refs):
    received, outs = refs[keeps_amount], refs[keeps_amount + 1 :]
    for slot in range(keeps_amount):
        summed = refs[slot][...] + received[slot].astype(F32)
        outs[slot][...] = summed.astype(outs[slot].dtype)


def parts_kernel(amount, *refs):
    out = refs[-1]
    half = out.shape[0] - 16
    values = [ref[...].astype(F32) for ref in refs[:amount]]
    while len(values) > 1:
        values = [values[i] + values[i + 1] for i in range(0, len(values), 2)]
    (total,) = values
    bias = total[half : half + 8] + total[half + 8 :]
    high, low = halves(bias)
    out[pl.ds(0, half), :] = total[:half].astype(out.dtype)
    if out.dtype == F32:
        high, low = bias, jnp.zeros_like(bias)
    out[pl.ds(half, 16), :] = jnp.concatenate([high.astype(F32), low.astype(F32)]).astype(out.dtype)


def finish_kernel(core, kept, *refs):
    arrived, refs = refs[:-6], refs[-6:]
    weight, part, part_other, grad_features, grad_weight, grad_bias = refs
    total = kept[...]
    for piece in arrived:
        total += piece[...].astype(F32)
    grad_features[...] = lax.dot_general(
        total.T.astype(BF16), weight[...], (((1,), (1,)), ((), ())), preferred_element_type=F32
    ).astype(BF16)
    half = part_other.shape[0]
    grad_weight[pl.ds(pl.multiple_of(core[0] * half, half), half), :] = part[pl.ds(0, half), :]
    grad_weight[pl.ds(pl.multiple_of((1 - core[0]) * half, half), half), :] = part_other[...]
    grad_bias[...] = part[pl.ds(half, 1), :]


def on_device(features, weight, bias, tiles, tile_col, live_tiles, cotangent):
    side, width = features.shape
    slots = tiles.shape[0]
    count = lax.axis_size("row")
    pairs = count // 2
    me = lax.axis_index("row").astype(jnp.int32)
    core = jnp.bitwise_and(me, 1)

    def swap(x, bit):
        return lax.ppermute(x, "row", [(i, i ^ bit) for i in range(count)])

    block = (side, width)
    wide = jax.ShapeDtypeStruct(block, F32)
    wide_t = jax.ShapeDtypeStruct((width, side), F32)
    zs = list(range(count - 4, -4, -4))
    gathered = {0: features}
    for z in zs[:-1] + [2]:
        gathered[z] = swap(features, z)
    def merge(parity, pieces):
        return call(
            functools.partial(merge_kernel, parity),
            [jax.ShapeDtypeStruct((pairs // pieces, side, side), BF16)] * pieces,
            (tile_col[0], live_tiles, me[None], tiles),
            in_specs=[SMEM, SMEM, SMEM, pl.BlockSpec(memory_space=pl.ANY)],
            scratch=[
                pltpu.VMEM((slots, side, side), BF16),
                pltpu.SMEM((count,), jnp.int32),
                pltpu.SMEM((slots,), jnp.int32),
                pltpu.SemaphoreType.DMA((slots,)),
            ],
            flops=slots * side * side,
            moved=slots * side * side,
            limit=48,
        )

    (own,) = merge(0, 1)
    sent_other = merge(1, PIECES)
    for z in zs[:-1]:
        gathered[z + 2] = swap(gathered[2], z) if z == 4 else swap(gathered[z], 2)
    other = [swap(piece, 1) for piece in sent_other]
    xs = [gathered[2 * index] for index in range(pairs)]
    mine, partner = call(
        aggregate_kernel,
        [wide] * 2,
        (own, *other, *xs),
        flops=4 * pairs * side**2 * width,
        moved=3 * pairs * side * width * 2,
    )
    received = swap(partner, 1)
    activation, grad, grad_bias = call(
        layer_kernel,
        [
            jax.ShapeDtypeStruct(block, BF16),
            jax.ShapeDtypeStruct((width, side), BF16),
            jax.ShapeDtypeStruct((8, width), F32),
        ],
        (mine, received, weight, bias[None, :], cotangent),
        flops=4 * side * width**2,
        moved=side * width * 16,
    )
    grad_other = swap(grad, 1)
    half = jax.ShapeDtypeStruct((width // 2 + 16, width), F32)
    part, part_send = call(
        weight_kernel,
        [half] * 2,
        (core[None], mine, received, grad, grad_bias),
        in_specs=[SMEM] + [VMEM] * 4,
        scratch=[pltpu.VMEM((width, width), F32)],
        flops=4 * side * width**2,
        moved=side * width * 12,
    )

    def add_parts(pieces, dtype, later=()):
        return call(
            functools.partial(parts_kernel, len(pieces)),
            jax.ShapeDtypeStruct(half.shape, dtype),
            (*pieces, *later),
            in_specs=[VMEM] * len(pieces) + [pl.BlockSpec(memory_space=pl.ANY)] * len(later),
            flops=len(pieces) * width**2,
            moved=len(pieces) * width**2,
        )

    share = max(1, len(zs) // 4)
    groups = [zs[start : start + share] for start in range(0, len(zs), share)]
    outs = call(
        functools.partial(backward_kernel, groups),
        [jax.ShapeDtypeStruct((len(group), width, side), BF16) for group in groups]
        + [wide_t] * len(zs),
        (own, grad, grad_other, *other),
        flops=4 * pairs * side**2 * width,
        moved=3 * pairs * side * width * 2,
    )
    sends, keeps = outs[: len(groups)], outs[len(groups) :]
    from_y = [swap(send, 2) for send in sends]
    packed = add_parts((part, swap(part_send, 1)), BF16, outs[:1])
    packed = add_parts([swap(packed, z) if z else packed for z in reversed(zs)], BF16)
    part = add_parts((packed, swap(packed, 2)), F32)
    arrived = []
    place = 0
    for index, group in enumerate(groups):
        summed = call(
            functools.partial(join_kernel, len(group)),
            [jax.ShapeDtypeStruct((width, side), BF16 if z else F32) for z in group],
            [*keeps[place : place + len(group)], from_y[index]],
            flops=len(group) * side * width,
            moved=len(group) * side * width * 8,
        )
        arrived += [swap(piece, z) if z else piece for piece, z in zip(summed, group)]
        place += len(group)
    part_other = swap(part[: width // 2], 1)
    grad_features, grad_weight, grad_bias = call(
        finish_kernel,
        [
            jax.ShapeDtypeStruct(block, BF16),
            jax.ShapeDtypeStruct((width, width), F32),
            jax.ShapeDtypeStruct((1, width), F32),
        ],
        (core[None], arrived[-1], *arrived[:-1], weight, part, part_other),
        in_specs=[SMEM] + [VMEM] * (len(zs) + 3),
        flops=2 * side * width**2,
        moved=side * width * 2 * (len(zs) + 4),
    )
    return activation, grad_features, grad_weight, grad_bias[0]


def solution(mesh):
    placed = (
        P(("parts", "row"), None),
        P(),
        P(),
        P(("parts", "row"), None, None),
        P(("parts", "row"), None),
        P(("parts", "row")),
        P(("parts", "row"), None),
    )
    return jax.shard_map(
        on_device,
        mesh=mesh,
        in_specs=placed,
        out_specs=(
            P(("parts", "row"), None),
            P(("parts", "row"), None),
            P("parts", None),
            P("parts"),
        ),
        check_vma=False,
    )
```

```python
import functools

import jax
import jax.numpy as jnp
from jax import lax
from jax.experimental import pallas as pl
from jax.experimental.pallas import tpu as pltpu
from jax.sharding import PartitionSpec as P

F32 = jnp.float32
BF16 = jnp.bfloat16
VMEM = pl.BlockSpec(memory_space=pltpu.VMEM)
SMEM = pl.BlockSpec(memory_space=pltpu.SMEM)
MIB = 1024 * 1024
PIECES = 8


def dot(a, b):
    return jnp.dot(a, b, preferred_element_type=F32)


def halves(x):
    high = x.astype(BF16)
    return high, (x - high.astype(F32)).astype(BF16)


def at(pieces, index):
    depth = pieces[0].shape[0]
    return pieces[index // depth][index % depth]


def call(kernel, out_shape, args, in_specs=None, scratch=(), flops=0, moved=0, limit=8):
    many = isinstance(out_shape, (list, tuple))
    return pl.pallas_call(
        kernel,
        out_shape=out_shape,
        in_specs=in_specs or [VMEM] * len(args),
        out_specs=[VMEM] * len(out_shape) if many else VMEM,
        scratch_shapes=list(scratch),
        compiler_params=pltpu.CompilerParams(vmem_limit_bytes=limit * MIB),
        cost_estimate=pl.CostEstimate(flops=flops, bytes_accessed=moved, transcendentals=0),
    )(*args)


def merge_kernel(parity, columns, live, me, tiles, *refs):
    outs, (head, following) = refs[:-2], refs[-2:]
    depth, side = outs[0].shape[:2]
    strip = side // 4

    def clear(index, carry):
        head[index] = -1
        return carry

    lax.fori_loop(0, head.shape[0], clear, 0)

    def link(slot, carry):
        where = lax.bitwise_xor(columns[slot], me[0])
        following[slot] = head[where]
        head[where] = slot
        return carry

    lax.fori_loop(0, live[0], link, 0)

    def fill(base, out, index, carry):
        for part in range(4):
            rows = pl.ds(part * strip, strip)

            def add(state, rows=rows):
                slot, total = state
                return following[slot], total + tiles[slot, rows, :].astype(F32)

            first = (head[2 * index + base], jnp.zeros((strip, side), F32))
            total = lax.while_loop(lambda state: state[0] >= 0, add, first)[1]
            out[index, rows, :] = total.astype(BF16)
        return carry

    for piece, out in enumerate(outs):
        base = parity + 2 * depth * piece
        lax.fori_loop(0, depth, functools.partial(fill, base, out), 0)


def aggregate_kernel(own, *refs):
    xs, (mine, partner) = refs[PIECES:-2], refs[-2:]
    total_mine = jnp.zeros(mine.shape, F32)
    total_partner = jnp.zeros(mine.shape, F32)
    for index, x in enumerate(xs):
        total_mine += dot(own[index], x[...])
        total_partner += dot(at(refs[:PIECES], index), x[...])
    mine[...] = total_mine
    partner[...] = total_partner


def layer_kernel(mine, received, weight, bias, cotangent, activation, grad_pre_t, grad_bias):
    high, low = halves(mine[...] + received[...])
    pre = dot(high, weight[...]) + dot(low, weight[...]) + bias[...]
    sigma = jax.nn.sigmoid(pre)
    activation[...] = (pre * sigma).astype(BF16)
    grad = (cotangent[...].astype(F32) * sigma * (1.0 + pre * (1.0 - sigma))).astype(BF16)
    grad = grad.astype(F32)
    grad_bias[...] = jnp.broadcast_to(jnp.sum(grad, axis=0, keepdims=True), grad_bias.shape)
    grad_pre_t[...] = grad.T.astype(BF16)


def weight_kernel(core, mine, received, grad, grad_bias, keep, send, whole):
    high, low = halves(mine[...] + received[...])
    whole[...] = (dot(grad[...], high) + dot(grad[...], low)).T
    half = keep.shape[0] - 16
    for out, which in ((keep, core[0]), (send, 1 - core[0])):
        out[pl.ds(0, half), :] = whole[pl.ds(pl.multiple_of(which * half, half), half), :]
        out[pl.ds(half, 8), :] = grad_bias[...]
        out[pl.ds(half + 8, 8), :] = jnp.zeros_like(grad_bias)


def backward_kernel(groups, own, grad, grad_other, *refs):
    other, refs = refs[:PIECES], refs[PIECES:]
    sends, keeps = refs[: len(groups)], refs[len(groups) :]
    g, go = grad[...], grad_other[...]
    place = 0
    for send, group in zip(sends, groups):
        for slot, z in enumerate(group):
            near, far = z // 2, z // 2 + 1
            send[slot] = (dot(g, own[far]) + dot(go, at(other, far))).astype(BF16)
            keeps[place][...] = dot(g, own[near]) + dot(go, at(other, near))
            place += 1


def join_kernel(keeps_amount, *refs):
    received, outs = refs[keeps_amount], refs[keeps_amount + 1 :]
    for slot in range(keeps_amount):
        summed = refs[slot][...] + received[slot].astype(F32)
        outs[slot][...] = summed.astype(outs[slot].dtype)


def parts_kernel(amount, *refs):
    out = refs[-1]
    half = out.shape[0] - 16
    values = [ref[...].astype(F32) for ref in refs[:amount]]
    while len(values) > 1:
        values = [values[i] + values[i + 1] for i in range(0, len(values), 2)]
    (total,) = values
    bias = total[half : half + 8] + total[half + 8 :]
    high, low = halves(bias)
    out[pl.ds(0, half), :] = total[:half].astype(out.dtype)
    if out.dtype == F32:
        high, low = bias, jnp.zeros_like(bias)
    out[pl.ds(half, 16), :] = jnp.concatenate([high.astype(F32), low.astype(F32)]).astype(out.dtype)


def finish_kernel(core, kept, *refs):
    arrived, refs = refs[:-6], refs[-6:]
    weight, part, part_other, grad_features, grad_weight, grad_bias = refs
    total = kept[...]
    for piece in arrived:
        total += piece[...].astype(F32)
    grad_features[...] = lax.dot_general(
        total.T.astype(BF16), weight[...], (((1,), (1,)), ((), ())), preferred_element_type=F32
    ).astype(BF16)
    half = part_other.shape[0]
    grad_weight[pl.ds(pl.multiple_of(core[0] * half, half), half), :] = part[pl.ds(0, half), :]
    grad_weight[pl.ds(pl.multiple_of((1 - core[0]) * half, half), half), :] = part_other[...]
    grad_bias[...] = part[pl.ds(half, 1), :]


def on_device(features, weight, bias, tiles, tile_col, live_tiles, cotangent):
    side, width = features.shape
    slots = tiles.shape[0]
    count = lax.axis_size("row")
    pairs = count // 2
    me = lax.axis_index("row").astype(jnp.int32)
    core = jnp.bitwise_and(me, 1)

    def swap(x, bit):
        return lax.ppermute(x, "row", [(i, i ^ bit) for i in range(count)])

    block = (side, width)
    wide = jax.ShapeDtypeStruct(block, F32)
    wide_t = jax.ShapeDtypeStruct((width, side), F32)
    zs = list(range(count - 4, -4, -4))
    gathered = {0: features}
    for z in zs[:-1] + [2]:
        gathered[z] = swap(features, z)

    def merge(parity, pieces):
        return call(
            functools.partial(merge_kernel, parity),
            [jax.ShapeDtypeStruct((pairs // pieces, side, side), BF16)] * pieces,
            (tile_col[0], live_tiles, me[None], tiles),
            in_specs=[SMEM, SMEM, SMEM, VMEM],
            scratch=[pltpu.SMEM((count,), jnp.int32), pltpu.SMEM((slots,), jnp.int32)],
            flops=slots * side * side,
            moved=slots * side * side,
            limit=20,
        )

    (own,) = merge(0, 1)
    sent_other = merge(1, PIECES)
    for z in zs[:-1]:
        gathered[z + 2] = swap(gathered[2], z) if z == 4 else swap(gathered[z], 2)
    other = [swap(piece, 1) for piece in sent_other]
    xs = [gathered[2 * index] for index in range(pairs)]
    mine, partner = call(
        aggregate_kernel,
        [wide] * 2,
        (own, *other, *xs),
        flops=4 * pairs * side**2 * width,
        moved=3 * pairs * side * width * 2,
    )
    received = swap(partner, 1)
    activation, grad, grad_bias = call(
        layer_kernel,
        [
            jax.ShapeDtypeStruct(block, BF16),
            jax.ShapeDtypeStruct((width, side), BF16),
            jax.ShapeDtypeStruct((8, width), F32),
        ],
        (mine, received, weight, bias[None, :], cotangent),
        flops=4 * side * width**2,
        moved=side * width * 16,
    )
    grad_other = swap(grad, 1)
    half = jax.ShapeDtypeStruct((width // 2 + 16, width), F32)
    part, part_send = call(
        weight_kernel,
        [half] * 2,
        (core[None], mine, received, grad, grad_bias),
        in_specs=[SMEM] + [VMEM] * 4,
        scratch=[pltpu.VMEM((width, width), F32)],
        flops=4 * side * width**2,
        moved=side * width * 12,
    )

    def add_parts(pieces, dtype, later=()):
        return call(
            functools.partial(parts_kernel, len(pieces)),
            jax.ShapeDtypeStruct(half.shape, dtype),
            (*pieces, *later),
            in_specs=[VMEM] * len(pieces) + [pl.BlockSpec(memory_space=pl.ANY)] * len(later),
            flops=len(pieces) * width**2,
            moved=len(pieces) * width**2,
        )

    share = max(1, len(zs) // 4)
    groups = [zs[start : start + share] for start in range(0, len(zs), share)]
    outs = call(
        functools.partial(backward_kernel, groups),
        [jax.ShapeDtypeStruct((len(group), width, side), BF16) for group in groups]
        + [wide_t] * len(zs),
        (own, grad, grad_other, *other),
        flops=4 * pairs * side**2 * width,
        moved=3 * pairs * side * width * 2,
    )
    sends, keeps = outs[: len(groups)], outs[len(groups) :]
    from_y = [swap(send, 2) for send in sends]
    arrived = []
    place = 0
    for index, group in enumerate(groups):
        summed = call(
            functools.partial(join_kernel, len(group)),
            [jax.ShapeDtypeStruct((width, side), BF16 if z else F32) for z in group],
            [*keeps[place : place + len(group)], from_y[index]],
            flops=len(group) * side * width,
            moved=len(group) * side * width * 8,
        )
        arrived += [swap(piece, z) if z else piece for piece, z in zip(summed, group)]
        place += len(group)
    packed = add_parts((part, swap(part_send, 1)), BF16, outs[:1])
    packed = add_parts([swap(packed, z) if z else packed for z in reversed(zs)], BF16)
    part = add_parts((packed, swap(packed, 2)), F32, arrived[:2])
    part_other = swap(part[: width // 2], 1)
    grad_features, grad_weight, grad_bias = call(
        finish_kernel,
        [
            jax.ShapeDtypeStruct(block, BF16),
            jax.ShapeDtypeStruct((width, width), F32),
            jax.ShapeDtypeStruct((1, width), F32),
        ],
        (core[None], arrived[-1], *arrived[:-1], weight, part, part_other),
        in_specs=[SMEM] + [VMEM] * (len(zs) + 3),
        flops=2 * side * width**2,
        moved=side * width * 2 * (len(zs) + 4),
    )
    return activation, grad_features, grad_weight, grad_bias[0]


def solution(mesh):
    placed = (
        P(("parts", "row"), None),
        P(),
        P(),
        P(("parts", "row"), None, None),
        P(("parts", "row"), None),
        P(("parts", "row")),
        P(("parts", "row"), None),
    )
    return jax.shard_map(
        on_device,
        mesh=mesh,
        in_specs=placed,
        out_specs=(
            P(("parts", "row"), None),
            P(("parts", "row"), None),
            P("parts", None),
            P("parts"),
        ),
        check_vma=False,
    )
```
